32 devices in a mesh: section: 2 (over x), row: 2 (over core), col: 4 (over z), dp: 2 (over y).
Axes of the slice: x: 2, y: 2, z: 4, core: 2. Of those that a mesh axis runs over, the one named last changes fastest.
Arguments:
- inputs: bfloat16 [2, 2, 512, 576], P('dp', None, 'col', 'row'), may hold values from -6 to 6
- segments: int32 [2, 2, 512], P('dp'), may hold values from 0 to 2, as said below
- cotangent: bfloat16 [2, 2, 512, 576], P('dp', None, 'col', 'row'), may hold values from -6 to 6
- gain_attn: bfloat16 [2, 576], P('section', 'row'), may hold values from 0.5 to 1.5
- w_query: bfloat16 [2, 576, 576], P('section', 'row', 'col'), may hold values from -0.25 to 0.25
- w_key: bfloat16 [2, 576, 192], P('section', 'row', 'col'), may hold values from -0.25 to 0.25
- w_value: bfloat16 [2, 576, 192], P('section', 'row', 'col'), may hold values from -0.25 to 0.25
- w_out: bfloat16 [2, 576, 576], P('section', 'col', 'row'), may hold values from -1.5 to 1.5
- gain_ffn: bfloat16 [2, 576], P('section', 'row'), may hold values from 0.5 to 1.5
- w_gate: bfloat16 [2, 576, 1536], P('section', 'row', 'col'), may hold values from -0.25 to 0.25
- w_up: bfloat16 [2, 576, 1536], P('section', 'row', 'col'), may hold values from -0.25 to 0.25
- w_down: bfloat16 [2, 1536, 576], P('section', 'col', 'row'), may hold values from -0.15625 to 0.15625
Outputs:
- activations: bfloat16 [2, 2, 2, 512, 576], P('section', 'dp', None, 'col', 'row')
- input_grads: float32 [2, 2, 2, 512, 576], P('section', 'dp', None, 'col', 'row')
- grad_gain_attn: float32 [2, 576], P('section', 'row')
- grad_w_query: float32 [2, 576, 576], P('section', 'row', 'col')
- grad_w_key: float32 [2, 576, 192], P('section', 'row', 'col')
- grad_w_value: float32 [2, 576, 192], P('section', 'row', 'col')
- grad_w_out: float32 [2, 576, 576], P('section', 'col', 'row')
- grad_gain_ffn: float32 [2, 576], P('section', 'row')
- grad_w_gate: float32 [2, 576, 1536], P('section', 'row', 'col')
- grad_w_up: float32 [2, 576, 1536], P('section', 'row', 'col')
- grad_w_down: float32 [2, 1536, 576], P('section', 'col', 'row')
The draws below stay inside these ranges and needn't reach their ends.
Inputs may be any that keep to these rules, and one draw needn't show every extreme that they name: `segments`: in each micro-batch the numbers never fall along the sequence and take each of the values 0, 1 and 2 on a run of one or more tokens; the run of 1 starts within the first 64 tokens and ends within the last 64.
All inputs are finite; a program needn't handle non-finite values.
Results may differ from the reference program's by a relative error of at most 0.02.
Values may be sent and summed in bfloat16 or wider, within the bound.
A program may use at most 128 MiB of HBM per device.

```python
import jax
import jax.numpy as jnp
from jax import lax

D = 576
HEADS = 9
KV_HEADS = 3
HEAD_DIM = 64
FF = 1536
TOK_DEV = 64
MB = 2
GROUPS = 2
SEQ = 512


def draw_segments(key, part):
    key = jax.random.fold_in(key, 7)
    key_start, key_stop = jax.random.split(key)
    opening = jax.random.randint(key_start, (GROUPS, MB, 1), 1, TOK_DEV)
    closing = jax.random.randint(key_stop, (GROUPS, MB, 1), SEQ - TOK_DEV + 1, SEQ)
    spots = jnp.arange(SEQ, dtype=jnp.int32)[None, None, :]
    return (spots >= opening).astype(jnp.int32) + (spots >= closing).astype(jnp.int32)


def block_levels(stream_key, shape, shards, low, largest):
    level = 1.0
    for position, parts in shards:
        draws = jax.random.uniform(jax.random.fold_in(jax.random.fold_in(stream_key, 6), position), (parts,), jnp.float32, low / len(shards), largest / len(shards))
        level = level * jnp.repeat(jnp.exp(draws), shape[position] // parts).reshape((-1,) + (1,) * (len(shape) - 1 - position))
    return level


def normal_values(stream_key, dims, spread, bound, cuts=(), kind=jnp.bfloat16):
    loudness = block_levels(stream_key, dims, cuts, -0.22, 0.18) if cuts else 1.0
    values = jax.random.normal(stream_key, dims, jnp.float32) * spread * loudness
    return jnp.minimum(jnp.maximum(values, -bound), bound).astype(kind)


def setup_inputs(seed: int = 0) -> dict:
    key_list = jax.random.split(jax.random.key(seed), 13)
    return {
        "inputs": normal_values(key_list[0], (GROUPS, MB, SEQ, D), 1.0, 6.0, ((0, 2), (2, 4), (3, 2))),
        "segments": draw_segments(jax.random.fold_in(key_list[12], 71), 0),
        "cotangent": normal_values(key_list[2], (GROUPS, MB, SEQ, D), 1.0, 6.0, ((0, 2), (2, 4), (3, 2))),
        "gain_attn": jnp.clip(1.0 + 0.1 * jax.random.normal(key_list[3], (2, D), jnp.float32), 0.5, 1.5).astype(jnp.bfloat16),
        "w_query": normal_values(key_list[4], (2, D, D), D ** -0.5, 0.25, ((0, 2), (1, 2), (2, 4))),
        "w_key": normal_values(key_list[5], (2, D, KV_HEADS * HEAD_DIM), D ** -0.5, 0.25, ((0, 2), (1, 2), (2, 4))),
        "w_value": normal_values(key_list[6], (2, D, KV_HEADS * HEAD_DIM), D ** -0.5, 0.25, ((0, 2), (1, 2), (2, 4))),
        "w_out": normal_values(key_list[7], (2, D, D), (max(D // 32, 1)) ** -0.5, 1.5, ((0, 2), (1, 4), (2, 2))),
        "gain_ffn": jnp.clip(1.0 + 0.1 * jax.random.normal(key_list[8], (2, D), jnp.float32), 0.5, 1.5).astype(jnp.bfloat16),
        "w_gate": normal_values(key_list[9], (2, D, FF), D ** -0.5, 0.25, ((0, 2), (1, 2), (2, 4))),
        "w_up": normal_values(key_list[10], (2, D, FF), D ** -0.5, 0.25, ((0, 2), (1, 2), (2, 4))),
        "w_down": normal_values(key_list[11], (2, FF, D), FF ** -0.5, 0.15625, ((0, 2), (1, 4), (2, 2))),
    }


EPS = 1e-05
THETA = 100000.0
HIGH = lax.Precision.HIGHEST

@jax.custom_vjp
def low(v):
    return lax.optimization_barrier(v.astype(jnp.bfloat16)).astype(jnp.float32)

@jax.custom_vjp
def low_back(v):
    return v

def low_keep(v):
    return (low(v), None)

def low_pass(kept, grad):
    return (grad,)

def back_keep(v):
    return (v, None)

def back_low(kept, grad):
    return (low(grad),)
low.defvjp(low_keep, low_pass)
low_back.defvjp(back_keep, back_low)

def matmul(left, right):
    return jnp.dot(left, right, precision=HIGH, preferred_element_type=jnp.float32)

def rms_norm(hidden, gain):
    return hidden * lax.rsqrt(lax.optimization_barrier(jnp.mean(hidden * hidden, axis=-1, keepdims=True)) + EPS) * gain

def rotate(vectors, cos_table, sin_table):
    half_dim = vectors.shape[-1] // 2
    turned = jnp.concatenate([-vectors[..., half_dim:], vectors[..., :half_dim]], axis=-1)
    return vectors * cos_table[:, None, :] + turned * sin_table[:, None, :]

def tables(segment_row):
    spots = jnp.arange(SEQ, dtype=jnp.int32)
    fresh = jnp.concatenate([jnp.ones((1,), dtype=bool), segment_row[1:] != segment_row[:-1]])
    starts = lax.cummax(jnp.where(fresh, spots, 0).astype(jnp.int32), axis=0)
    positions = (spots - starts).astype(jnp.float32)
    frequency = THETA ** (-jnp.arange(HEAD_DIM // 2, dtype=jnp.float32) * 2.0 / HEAD_DIM)
    angles = positions[:, None] * frequency[None, :]
    angles = jnp.concatenate([angles, angles], axis=1)
    allowed = (segment_row[:, None] == segment_row[None, :]) & (spots[None, :] <= spots[:, None])
    return (jnp.cos(angles), jnp.sin(angles), allowed)

def attention(queries, key_rows, value_rows, allowed):
    length = queries.shape[0]
    grouped = queries.reshape(length, KV_HEADS, HEADS // KV_HEADS, HEAD_DIM)

    def one_head(items):
        q_head, k_head, v_head = items
        scores = jnp.einsum('qgd,kd->gqk', q_head, k_head, precision=HIGH) * HEAD_DIM ** (-0.5)
        scores = low_back(scores)
        scores = jnp.where(allowed[None], scores, -1e+30)
        highest = lax.optimization_barrier(jnp.max(scores, axis=-1, keepdims=True))
        raised = jnp.exp(scores - highest)
        weights = low(raised / lax.optimization_barrier(jnp.sum(raised, axis=-1, keepdims=True)))
        return jnp.einsum('gqk,kd->qgd', weights, v_head, precision=HIGH)
    results = lax.map(jax.checkpoint(one_head), (grouped.transpose(1, 0, 2, 3), key_rows.transpose(1, 0, 2), value_rows.transpose(1, 0, 2)))
    return results.transpose(1, 0, 2, 3).reshape(length, -1)

def layer(hidden, gain_attn, w_query, w_key, w_value, w_out, gain_ffn, w_gate, w_up, w_down, cos_table, sin_table, allowed):
    length = hidden.shape[0]
    normed = low(rms_norm(hidden, gain_attn))
    queries = low(low_back(matmul(normed, w_query)))
    key_part = low(low_back(matmul(normed, w_key)))
    value_part = low(low_back(matmul(normed, w_value)))
    queries = low(rotate(queries.reshape(length, HEADS, HEAD_DIM), cos_table, sin_table))
    key_part = low(rotate(key_part.reshape(length, KV_HEADS, HEAD_DIM), cos_table, sin_table))
    value_part = value_part.reshape(length, KV_HEADS, HEAD_DIM)
    attended = low(low_back(attention(queries, key_part, value_part, allowed)))
    residual = hidden + low_back(matmul(attended, w_out))
    normed_ffn = low(rms_norm(residual, gain_ffn))
    gate_vals = low_back(matmul(normed_ffn, w_gate))
    up_vals = low_back(matmul(normed_ffn, w_up))
    inner = low(jax.nn.silu(gate_vals) * up_vals)
    return residual + low_back(matmul(inner, w_down))

def reference(inputs, segments, cotangent, gain_attn, w_query, w_key, w_value, w_out, gain_ffn, w_gate, w_up, w_down):
    params = (gain_attn, w_query, w_key, w_value, w_out, gain_ffn, w_gate, w_up, w_down)
    front = tuple((item[0].astype(jnp.float32) for item in params))
    behind = tuple((item[1].astype(jnp.float32) for item in params))
    flat_in = inputs.reshape(-1, SEQ, D)
    flat_seg = segments.reshape(-1, SEQ)
    flat_cot = cotangent.reshape(-1, SEQ, D)

    def per_sequence(totals, items):
        entry, segment_row, grad_out = items
        cos_table, sin_table, allowed = tables(segment_row)

        def run(hidden, *weights):
            return layer(hidden, *weights, cos_table, sin_table, allowed)
        out_front, back_front = jax.vjp(run, entry.astype(jnp.float32), *front)
        passed = low(out_front)
        out_behind, back_behind = jax.vjp(run, passed, *behind)
        grads_behind = back_behind(grad_out.astype(jnp.float32))
        grads_front = back_front(low(grads_behind[0]))
        new_front = tuple((left + right for left, right in zip(totals[0], grads_front[1:])))
        new_behind = tuple((left + right for left, right in zip(totals[1], grads_behind[1:])))
        return ((new_front, new_behind), (passed.astype(jnp.bfloat16), out_behind.astype(jnp.bfloat16), grads_front[0], grads_behind[0]))
    zeros = (tuple((jnp.zeros_like(item) for item in front)), tuple((jnp.zeros_like(item) for item in behind)))
    totals, outs = lax.scan(per_sequence, zeros, (flat_in, flat_seg, flat_cot))
    acts_front, acts_behind, grad_front, grad_behind = outs
    shape = inputs.shape
    activations = jnp.stack([acts_front.reshape(shape), acts_behind.reshape(shape)])
    input_grads = jnp.stack([grad_front.reshape(shape), grad_behind.reshape(shape)])
    stacked = tuple((jnp.stack([left, right]) for left, right in zip(totals[0], totals[1])))
    return (activations, input_grads, stacked[0], stacked[1], stacked[2], stacked[3], stacked[4], stacked[5], stacked[6], stacked[7], stacked[8])
```

```python
import functools

import jax
import jax.numpy as jnp
from jax import lax
from jax.experimental import pallas as pl
from jax.experimental.pallas import tpu as pltpu
from jax.sharding import PartitionSpec as P

HEADS = 9
KV_HEADS = 3
HEAD_DIM = 64
EPS = 1e-05
THETA = 100000.0
MESH = pl.DeviceIdType.MESH
F32 = jnp.float32
BF16 = jnp.bfloat16
VMEM_LIMIT = 56 * 1024 * 1024


def dot(left, right):
    return jnp.dot(left, right, preferred_element_type=F32)


def dot_tn(left, right):
    return lax.dot_general(left, right, (((0,), (0,)), ((), ())), preferred_element_type=F32)


def dot_nt(left, right):
    return lax.dot_general(left, right, (((1,), (1,)), ((), ())), preferred_element_type=F32)


def exchange(items, axis, collective_id):
    size = lax.axis_size(axis)
    count = len(items)

    def body(*refs):
        ins, outs = refs[:count], refs[count : 2 * count]
        send_sem, recv_sem, own_sem = refs[2 * count :]
        me = lax.axis_index(axis)
        barrier = pltpu.get_barrier_semaphore()
        for step in range(1, size):
            pl.semaphore_signal(
                barrier, inc=1, device_id={axis: lax.rem(me + step, size)}, device_id_type=MESH
            )
        pl.semaphore_wait(barrier, size - 1)

        def remote(no, step, target, slot):
            gather = items[no][1]
            return pltpu.make_async_remote_copy(
                src_ref=ins[no] if gather else ins[no].at[target],
                dst_ref=outs[no].at[slot],
                send_sem=send_sem.at[no, step - 1],
                recv_sem=recv_sem.at[no, step - 1],
                device_id={axis: target},
                device_id_type=MESH,
            )

        for step in range(1, size):
            for no in range(count):
                remote(no, step, lax.rem(me + step, size), me).start()
        local = [
            pltpu.make_async_copy(
                ins[no] if items[no][1] else ins[no].at[me], outs[no].at[me], own_sem.at[no]
            )
            for no in range(count)
        ]
        for copy in local:
            copy.start()
        for copy in local:
            copy.wait()
        for step in range(1, size):
            for no in range(count):
                source = lax.rem(me + size - step, size)
                remote(no, step, lax.rem(me + step, size), me).wait_send()
                remote(no, step, lax.rem(me + step, size), source).wait_recv()

    shapes = [
        jax.ShapeDtypeStruct((size,) + item.shape if gather else item.shape, item.dtype)
        for item, gather in items
    ]
    any_spec = pl.BlockSpec(memory_space=pl.ANY)
    return pl.pallas_call(
        body,
        out_shape=shapes,
        in_specs=[any_spec] * count,
        out_specs=[any_spec] * count,
        scratch_shapes=[
            pltpu.SemaphoreType.DMA((count, size - 1)),
            pltpu.SemaphoreType.DMA((count, size - 1)),
            pltpu.SemaphoreType.DMA((count,)),
        ],
        compiler_params=pltpu.CompilerParams(collective_id=collective_id, has_side_effects=True),
        name="exchange_%d" % collective_id,
    )(*[item for item, _ in items])


class Group:
    def __init__(self, rows_n, cols_n, send_sem, recv_sem):
        self.rows_n = rows_n
        self.size = rows_n * cols_n
        self.me = lax.axis_index("col") * rows_n + lax.axis_index("row")
        self.send_sem = send_sem
        self.recv_sem = recv_sem

    def peer(self, step):
        return lax.rem(self.me + step, self.size)

    def device(self, place):
        return {"col": place // self.rows_n, "row": lax.rem(place, self.rows_n)}

    def greet(self):
        barrier = pltpu.get_barrier_semaphore()
        for step in range(1, self.size):
            pl.semaphore_signal(
                barrier, inc=1, device_id=self.device(self.peer(step)), device_id_type=MESH
            )
        pl.semaphore_wait(barrier, self.size - 1)

    def block(self, ref, place, tokens):
        return ref.at[pl.ds(pl.multiple_of(place * tokens, tokens), tokens)]

    def copy(self, phase, step, src, dst):
        return pltpu.make_async_remote_copy(
            src_ref=src,
            dst_ref=dst,
            send_sem=self.send_sem.at[phase, step - 1],
            recv_sem=self.recv_sem.at[phase, step - 1],
            device_id=self.device(self.peer(step)),
            device_id_type=MESH,
        )

    def gather_start(self, phase, ref, tokens):
        own = self.block(ref, self.me, tokens)
        for step in range(1, self.size):
            self.copy(phase, step, own, own).start()

    def gather_wait(self, phase, ref, tokens):
        own = self.block(ref, self.me, tokens)
        for step in range(1, self.size):
            source = self.block(ref, self.peer(self.size - step), tokens)
            self.copy(phase, step, own, own).wait_send()
            self.copy(phase, step, own, source).wait_recv()

    def scatter_start(self, phase, ref, landing, tokens):
        for step in range(1, self.size):
            src = self.block(ref, self.peer(step), tokens)
            self.copy(phase, step, src, landing.at[step - 1]).start()

    def scatter_sum(self, phase, ref, landing, tokens):
        total = self.block(ref, self.me, tokens)[...].astype(F32)
        for step in range(1, self.size):
            src = self.block(ref, self.peer(step), tokens)
            copy = self.copy(phase, step, src, landing.at[step - 1])
            copy.wait_recv()
            total += landing[step - 1].astype(F32)
            copy.wait_send()
        return total


def turned(values):
    width = values.shape[1]
    lane = lax.broadcasted_iota(jnp.int32, values.shape, 1)
    first = lax.rem(lane, HEAD_DIM) < HEAD_DIM // 2
    ahead = pltpu.roll(values, width - HEAD_DIM // 2, 1)
    behind = pltpu.roll(values, HEAD_DIM // 2, 1)
    return jnp.where(first, -ahead, behind)


def three_heads(ref, base, group):
    start = base + group * 3 * HEAD_DIM
    return jnp.concatenate(
        [ref[:, start + h * HEAD_DIM : start + (h + 1) * HEAD_DIM] for h in range(3)], axis=0
    )


def probabilities(queries, keys, allowed):
    scores = dot_nt(queries, keys) * HEAD_DIM ** (-0.5)
    scores = jnp.where(allowed, scores, -1e30)
    raised = jnp.exp(scores - jnp.max(scores, axis=1, keepdims=True))
    return raised / jnp.sum(raised, axis=1, keepdims=True)


def allowed_pairs(own_seg, own_tok, all_seg):
    rows, length = own_seg.shape[0], all_seg.shape[1]
    spots = lax.broadcasted_iota(jnp.int32, (rows, length), 1)
    return (own_seg == all_seg) & (spots <= own_tok)


def forward_body(
    rows_n, cols_n,
    x_ref, gain_a, gain_f, wqkv, wout, wgu, wdn, cos, sin, own_seg, own_tok, all_seg,
    y_ref, a_ref, qkv_ref, kv_ref, o_ref, r_ref, b_ref, gu_ref, hid_ref,
    part, landing, send_sem, recv_sem,
):
    group = Group(rows_n, cols_n, send_sem, recv_sem)
    tokens, width = x_ref.shape
    kv_width = kv_ref.shape[1]
    ff = hid_ref.shape[1]
    group.greet()
    x = x_ref[...]
    scale = lax.rsqrt(jnp.mean(x * x, axis=1, keepdims=True) + EPS)
    a = (x * scale * gain_a[...]).astype(BF16)
    a_ref[...] = a
    raw = dot(a, wqkv[...]).astype(BF16).astype(F32)
    qkv_ref[...] = (raw * cos[...] + turned(raw) * sin[...]).astype(BF16)
    group.block(kv_ref, group.me, tokens)[...] = qkv_ref[:, :kv_width]
    group.gather_start(0, kv_ref, tokens)
    allowed = allowed_pairs(own_seg[...], own_tok[...], all_seg[...])
    group.gather_wait(0, kv_ref, tokens)
    half = kv_width // 2
    for g in range(KV_HEADS):
        keys = kv_ref[:, g * HEAD_DIM : (g + 1) * HEAD_DIM]
        values = kv_ref[:, half + g * HEAD_DIM : half + (g + 1) * HEAD_DIM]
        p = probabilities(three_heads(qkv_ref, kv_width, g), keys, allowed)
        out = dot(p.astype(BF16), values).astype(BF16)
        for h in range(3):
            at = (3 * g + h) * HEAD_DIM
            o_ref[:, at : at + HEAD_DIM] = out[h * tokens : (h + 1) * tokens]
    r = x + dot(o_ref[...], wout[...])
    r_ref[...] = r
    scale = lax.rsqrt(jnp.mean(r * r, axis=1, keepdims=True) + EPS)
    group.block(b_ref, group.me, tokens)[...] = (r * scale * gain_f[...]).astype(BF16)
    group.gather_start(1, b_ref, tokens)
    group.gather_wait(1, b_ref, tokens)
    gu_ref[...] = dot(b_ref[...], wgu[...])
    gate = gu_ref[:, :ff]
    hid_ref[...] = (gate / (1.0 + jnp.exp(-gate)) * gu_ref[:, ff:]).astype(BF16)
    part[...] = dot(hid_ref[...], wdn[...]).astype(BF16)
    group.scatter_start(2, part, landing, tokens)
    y_ref[...] = r_ref[...] + group.scatter_sum(2, part, landing, tokens)


def norm_back(x, gain, gz):
    scale = lax.rsqrt(jnp.mean(x * x, axis=1, keepdims=True) + EPS)
    weighted = gz * gain
    inner = jnp.mean(weighted * x, axis=1, keepdims=True)
    return (
        scale * weighted - x * (scale * scale * scale) * inner,
        jnp.sum(gz * x * scale, axis=0, keepdims=True),
    )


def backward_body(
    rows_n, cols_n,
    gy_ref, x_ref, gain_a, gain_f, wqkv, wout, wgu, wdn, cos, sin, own_seg, own_tok, all_seg,
    a_ref, qkv_ref, kv_ref, o_ref, r_ref, b_ref, gu_ref, hid_ref,
    gx_ref, gwqkv, gwout, gwgu, gwdn, ggain_a, ggain_f,
    gf_ref, ggu_ref, part, landing, kv_part, kv_landing, go_ref, gq_ref, gr_ref,
    send_sem, recv_sem,
):
    group = Group(rows_n, cols_n, send_sem, recv_sem)
    tokens, width = x_ref.shape
    kv_width = kv_ref.shape[1]
    half = kv_width // 2
    ff = hid_ref.shape[1]
    group.greet()
    group.block(gf_ref, group.me, tokens)[...] = gy_ref[...].astype(BF16)
    group.gather_start(0, gf_ref, tokens)
    group.gather_wait(0, gf_ref, tokens)
    ghid = dot_nt(gf_ref[...], wdn[...])
    gate = gu_ref[:, :ff]
    sig = 1.0 / (1.0 + jnp.exp(-gate))
    ggu_ref[:, :ff] = (ghid * gu_ref[:, ff:] * (sig * (1.0 + gate * (1.0 - sig)))).astype(BF16)
    ggu_ref[:, ff:] = (ghid * (gate * sig)).astype(BF16)
    part[...] = dot_nt(ggu_ref[...], wgu[...]).astype(BF16)
    group.scatter_start(1, part, landing, tokens)
    gwdn[...] = dot_tn(hid_ref[...], gf_ref[...]).astype(BF16)
    gwgu[...] = dot_tn(b_ref[...], ggu_ref[...]).astype(BF16)
    gb = group.scatter_sum(1, part, landing, tokens)
    grad, ggain_f[...] = norm_back(r_ref[...], gain_f[...], gb)
    gr = gy_ref[...] + grad
    gr_ref[...] = gr
    grad_b = gr.astype(BF16)
    go_ref[...] = dot_nt(grad_b, wout[...]).astype(BF16)
    allowed = allowed_pairs(own_seg[...], own_tok[...], all_seg[...])
    factor = HEAD_DIM ** (-0.5)
    gq_ref[...] = jnp.zeros_like(gq_ref)
    for g in range(KV_HEADS):
        keys = kv_ref[:, g * HEAD_DIM : (g + 1) * HEAD_DIM]
        values = kv_ref[:, half + g * HEAD_DIM : half + (g + 1) * HEAD_DIM]
        queries = three_heads(qkv_ref, kv_width, g)
        gout = three_heads(go_ref, 0, g)
        p = probabilities(queries, keys, allowed)
        gp = dot_nt(gout, values)
        gs = (p * (gp - jnp.sum(gp * p, axis=1, keepdims=True))).astype(BF16)
        gq = dot(gs, keys) * factor
        for h in range(3):
            at = kv_width + (3 * g + h) * HEAD_DIM
            gq_ref[:, at : at + HEAD_DIM] = gq[h * tokens : (h + 1) * tokens]
        at = g * HEAD_DIM
        kv_part[:, at : at + HEAD_DIM] = (dot_tn(gs, queries) * factor).astype(BF16)
        kv_part[:, half + at : half + at + HEAD_DIM] = dot_tn(p.astype(BF16), gout).astype(BF16)
    group.scatter_start(2, kv_part, kv_landing, tokens)
    gwout[...] = dot_tn(o_ref[...], gr_ref[...].astype(BF16)).astype(BF16)
    gq_ref[:, :kv_width] = group.scatter_sum(2, kv_part, kv_landing, tokens)
    g0 = gq_ref[...]
    packed = (g0 * cos[...] - turned(g0 * sin[...])).astype(BF16)
    ga = dot_nt(packed, wqkv[...])
    gwqkv[...] = dot_tn(a_ref[...], packed).astype(BF16)
    grad, ggain_a[...] = norm_back(x_ref[...], gain_a[...], ga)
    gx_ref[...] = gr_ref[...] + grad


def call_layer(body, operands, out_shapes, scratch, rows_n, cols_n, phases, collective_id, name):
    size = rows_n * cols_n
    spec = pl.BlockSpec(memory_space=pltpu.VMEM)
    return pl.pallas_call(
        functools.partial(body, rows_n, cols_n),
        out_shape=[jax.ShapeDtypeStruct(shape, kind) for shape, kind in out_shapes],
        in_specs=[spec] * len(operands),
        out_specs=[spec] * len(out_shapes),
        scratch_shapes=[pltpu.VMEM(shape, kind) for shape, kind in scratch]
        + [pltpu.SemaphoreType.DMA((phases, size - 1))] * 2,
        compiler_params=pltpu.CompilerParams(
            collective_id=collective_id, has_side_effects=True, vmem_limit_bytes=VMEM_LIMIT
        ),
        name=name,
    )(*operands)


def tables(segment_row, offset, row_count, kv_width, padded, used):
    own_ids = lax.dynamic_slice_in_dim(segment_row, offset, row_count)
    token_ids = offset + jnp.arange(row_count, dtype=jnp.int32)
    starts = jnp.sum((segment_row[None, :] < own_ids[:, None]).astype(jnp.int32), axis=1)
    positions = (token_ids - starts).astype(F32)
    frequency = THETA ** (-jnp.arange(HEAD_DIM // 2, dtype=F32) * 2.0 / HEAD_DIM)
    angles = positions[:, None] * frequency[None, :]
    lanes = jnp.arange(padded)
    turns = (lanes < kv_width // 2) | ((lanes >= kv_width) & (lanes < used))
    repeat = padded // (HEAD_DIM // 2)
    cos = jnp.where(turns[None, :], jnp.tile(jnp.cos(angles), (1, repeat)), 1.0)
    sin = jnp.where(turns[None, :], jnp.tile(jnp.sin(angles), (1, repeat)), 0.0)
    return cos, sin, jnp.tile(own_ids, 3)[:, None], jnp.tile(token_ids, 3)[:, None]


def on_device(
    inputs, segments, cotangent, gain_attn, w_query, w_key, w_value, w_out, gain_ffn,
    w_gate, w_up, w_down,
):
    rows_n, cols_n = lax.axis_size("row"), lax.axis_size("col")
    section = lax.axis_index("section")
    size = rows_n * cols_n
    length = segments.shape[2]
    tokens = length // size
    band = w_query.shape[1]
    width = band * rows_n
    qc, kc = w_query.shape[2], w_key.shape[2]
    kv_width = 2 * kc * cols_n
    used = kv_width + qc * cols_n
    padded = -(-used // 128) * 128
    fc = w_gate.shape[2] // rows_n
    fp = -(-fc // 128) * 128

    qkv = jnp.concatenate([w_key[0], w_value[0], w_query[0]], axis=1)
    gate_up = jnp.stack(
        [w_gate[0].reshape(band, rows_n, fc), w_up[0].reshape(band, rows_n, fc)], axis=2
    ).transpose(1, 0, 2, 3).reshape(rows_n, band, 2 * fc)
    down = w_down[0].reshape(rows_n, fc, band)
    gains = jnp.stack([gain_attn[0], gain_ffn[0]])
    qkv, out, gate_up, down, gains = exchange(
        [(qkv, True), (w_out[0], True), (gate_up, True), (down, True), (gains, True)], "section", 0
    )
    qkv, out = exchange([(qkv, True), (out, True)], "col", 1)
    mine = lax.dynamic_index_in_dim(inputs[0], section, 0, False).reshape(rows_n, tokens, band)
    cot = lax.dynamic_index_in_dim(cotangent[0], section, 0, False).reshape(rows_n, tokens, band)
    qkv, out, gate_up, down, gains, mine, cot = exchange(
        [
            (qkv, True), (out, True),
            (gate_up.transpose(1, 0, 2, 3), False), (down.transpose(1, 0, 2, 3), False),
            (gains, True), (mine, False), (cot, False),
        ],
        "row", 2,
    )
    layers = gains.shape[1]
    pad = jnp.zeros((width, padded - used), BF16)
    full = []
    for n in range(layers):
        part = qkv[:, :, n].transpose(0, 2, 1, 3)
        part = jnp.concatenate(
            [
                part[..., :kc].reshape(width, -1),
                part[..., kc : 2 * kc].reshape(width, -1),
                part[..., 2 * kc :].reshape(width, -1),
                pad,
            ],
            axis=1,
        )
        wout = out[:, :, n].transpose(1, 2, 0, 3).reshape(width, width)
        wgu = jnp.pad(
            gate_up[:, n].reshape(width, 2, fc), ((0, 0), (0, 0), (0, fp - fc))
        ).reshape(width, 2 * fp)
        wdn = jnp.pad(
            down[:, n].transpose(1, 0, 2).reshape(fc, width), ((0, fp - fc), (0, 0))
        )
        gain = gains[:, n].transpose(1, 0, 2).reshape(2, 1, width).astype(F32)
        full.append((gain[0], gain[1], part, wout, wgu, wdn))

    segment_row = lax.dynamic_index_in_dim(segments[0], section, 0, False)
    place = lax.axis_index("col") * rows_n + lax.axis_index("row")
    cos, sin, own_seg, own_tok = tables(
        segment_row, place * tokens, tokens, kv_width, padded, used
    )
    table_set = (cos, sin, own_seg, own_tok, segment_row[None, :])

    entry = mine.transpose(1, 0, 2).reshape(tokens, width).astype(F32)
    saved, acts = [], []
    for n in range(layers):
        y, *kept = call_layer(
            forward_body,
            (entry, *full[n], *table_set),
            [
                ((tokens, width), F32), ((tokens, width), BF16), ((tokens, padded), BF16),
                ((length, kv_width), BF16), ((tokens, width), BF16), ((tokens, width), F32),
                ((length, width), BF16), ((length, 2 * fp), F32), ((length, fp), BF16),
            ],
            [((length, width), BF16), ((size - 1, tokens, width), BF16)],
            rows_n, cols_n, 3, 3, "layer_forward",
        )
        saved.append((entry, kept))
        acts.append(y.astype(BF16))
        entry = acts[-1].astype(F32)

    grad = cot.transpose(1, 0, 2).reshape(tokens, width).astype(F32)
    grads, weight_grads = [None] * layers, [None] * layers
    for n in reversed(range(layers)):
        entry, kept = saved[n]
        grads[n], *weight_grads[n] = call_layer(
            backward_body,
            (grad, entry, *full[n], *table_set, *kept),
            [
                ((tokens, width), F32), ((width, padded), BF16), ((width, width), BF16),
                ((width, 2 * fp), BF16), ((fp, width), BF16), ((1, width), F32), ((1, width), F32),
            ],
            [
                ((length, width), BF16), ((length, 2 * fp), BF16), ((length, width), BF16),
                ((size - 1, tokens, width), BF16), ((length, kv_width), BF16),
                ((size - 1, tokens, kv_width), BF16), ((tokens, width), BF16),
                ((tokens, padded), F32), ((tokens, width), F32),
            ],
            rows_n, cols_n, 3, 4, "layer_backward",
        )
        grad = grads[n].astype(BF16).astype(F32)

    def qkv_blocks(item):
        key, value, query = (
            item[:, at : at + cols_n * cut].reshape(rows_n, band, cols_n, cut)
            for at, cut in ((0, kc), (kv_width // 2, kc), (kv_width, qc))
        )
        return jnp.concatenate([key, value, query], axis=3).transpose(0, 2, 1, 3)

    g_qkv = jnp.stack([qkv_blocks(item[0]) for item in weight_grads], axis=1)
    out_rows = width // cols_n
    g_out = jnp.stack(
        [
            item[1].reshape(cols_n, out_rows, rows_n, band).transpose(2, 0, 1, 3)
            for item in weight_grads
        ],
        axis=1,
    )
    g_gu = jnp.stack(
        [
            item[2].reshape(rows_n, band, 2, fp)[..., :fc].reshape(rows_n, band, 2 * fc)
            for item in weight_grads
        ],
        axis=1,
    )
    g_dn = jnp.stack(
        [item[3][:fc].reshape(fc, rows_n, band).transpose(1, 0, 2) for item in weight_grads],
        axis=1,
    )
    g_gain = jnp.stack(
        [jnp.stack([item[4], item[5]]).reshape(2, rows_n, band) for item in weight_grads]
    ).transpose(2, 0, 1, 3)
    act = jnp.stack(acts).reshape(layers, tokens, rows_n, band).transpose(2, 0, 1, 3)
    in_grad = jnp.stack(grads).reshape(layers, tokens, rows_n, band).transpose(2, 0, 1, 3)
    g_qkv, g_out, g_gu, g_dn, g_gain, act, in_grad = exchange(
        [(item, False) for item in (g_qkv, g_out, g_gu, g_dn, g_gain, act, in_grad)], "row", 5
    )

    def add(item):
        return jnp.sum(item.astype(F32), axis=0)

    g_qkv, g_out, g_gu, g_dn, g_gain, act, in_grad = exchange(
        [
            (add(g_qkv).astype(BF16), False), (add(g_out).astype(BF16), False),
            (g_gu.transpose(1, 0, 2, 3), False), (g_dn.transpose(1, 0, 2, 3), False),
            (add(g_gain), False),
            (act.transpose(1, 0, 2, 3), False), (in_grad.transpose(1, 0, 2, 3), False),
        ],
        "section", 6,
    )
    activations = act.reshape((1, 1) + inputs.shape[1:])
    input_grads = in_grad.reshape((1, 1) + inputs.shape[1:])
    g_qkv, g_out, g_gain = exchange(
        [(add(g_qkv).astype(BF16), False), (add(g_out).astype(BF16), False), (add(g_gain), True)],
        "col", 7,
    )
    g_qkv, g_out, g_gu, g_dn, g_gain = (
        add(item)
        for item in exchange(
            [
                (add(g_qkv).astype(BF16), True), (add(g_out).astype(BF16), True),
                (add(g_gu).astype(BF16), True), (add(g_dn).astype(BF16), True),
                (add(g_gain), True),
            ],
            "dp", 8,
        )
    )
    g_gu = g_gu.reshape(rows_n, band, 2, fc).transpose(2, 1, 0, 3).reshape(2, band, rows_n * fc)
    return (
        activations, input_grads, g_gain[0][None], g_qkv[:, 2 * kc :][None], g_qkv[:, :kc][None],
        g_qkv[:, kc : 2 * kc][None], g_out[None], g_gain[1][None], g_gu[0][None], g_gu[1][None],
        g_dn.reshape(rows_n * fc, band)[None],
    )


def solution(mesh):
    grid = P("section", "row", "col")
    turned_grid = P("section", "col", "row")
    gain = P("section", "row")
    tokens = P("dp", None, "col", "row")
    result = P("section", "dp", None, "col", "row")
    weights = (gain, grid, grid, grid, turned_grid, gain, grid, grid, turned_grid)
    return jax.shard_map(
        on_device,
        mesh=mesh,
        in_specs=(tokens, P("dp", None, None), tokens) + weights,
        out_specs=(result, result) + weights,
        check_vma=False,
    )
```

```python
import functools

import jax
import jax.numpy as jnp
from jax import lax
from jax.experimental import pallas as pl
from jax.experimental.pallas import tpu as pltpu
from jax.sharding import PartitionSpec as P

HEADS = 9
KV_HEADS = 3
HEAD_DIM = 64
EPS = 1e-05
THETA = 100000.0
MESH = pl.DeviceIdType.MESH
F32 = jnp.float32
BF16 = jnp.bfloat16
VMEM_LIMIT = 56 * 1024 * 1024


def dot(left, right):
    return jnp.dot(left, right, preferred_element_type=F32)


def dot_tn(left, right):
    return lax.dot_general(left, right, (((0,), (0,)), ((), ())), preferred_element_type=F32)


def dot_nt(left, right):
    return lax.dot_general(left, right, (((1,), (1,)), ((), ())), preferred_element_type=F32)


def exchange(items, collective_id):
    count = len(items)
    axes = sorted({axis for _, axis, _ in items})
    most = max(lax.axis_size(axis) for axis in axes) - 1

    def body(*refs):
        ins, outs = refs[:count], refs[count : 2 * count]
        send_sem, recv_sem, own_sem = refs[2 * count :]
        barrier = pltpu.get_barrier_semaphore()

        def other(axis, step):
            size = lax.axis_size(axis)
            return lax.rem(lax.axis_index(axis) + step + size, size)

        for axis in axes:
            for step in range(1, lax.axis_size(axis)):
                pl.semaphore_signal(
                    barrier, inc=1, device_id={axis: other(axis, step)}, device_id_type=MESH
                )
        pl.semaphore_wait(barrier, sum(lax.axis_size(axis) - 1 for axis in axes))

        def remote(no, step, slot):
            _, axis, gather = items[no]
            target = other(axis, step)
            return pltpu.make_async_remote_copy(
                src_ref=ins[no] if gather else ins[no].at[target],
                dst_ref=outs[no].at[slot],
                send_sem=send_sem.at[no, step - 1],
                recv_sem=recv_sem.at[no, step - 1],
                device_id={axis: target},
                device_id_type=MESH,
            )

        for no, (_, axis, gather) in enumerate(items):
            for step in range(1, lax.axis_size(axis)):
                remote(no, step, lax.axis_index(axis)).start()
        local = []
        for no, (_, axis, gather) in enumerate(items):
            me = lax.axis_index(axis)
            src = ins[no] if gather else ins[no].at[me]
            local.append(pltpu.make_async_copy(src, outs[no].at[me], own_sem.at[no]))
        for copy in local:
            copy.start()
        for copy in local:
            copy.wait()
        for no, (_, axis, gather) in enumerate(items):
            for step in range(1, lax.axis_size(axis)):
                remote(no, step, lax.axis_index(axis)).wait_send()
                remote(no, step, other(axis, -step)).wait_recv()

    shapes = [
        jax.ShapeDtypeStruct(
            (lax.axis_size(axis),) + item.shape if gather else item.shape, item.dtype
        )
        for item, axis, gather in items
    ]
    spec = pl.BlockSpec(memory_space=pltpu.VMEM)
    return pl.pallas_call(
        body,
        out_shape=shapes,
        in_specs=[spec] * count,
        out_specs=[spec] * count,
        scratch_shapes=[
            pltpu.SemaphoreType.DMA((count, most)),
            pltpu.SemaphoreType.DMA((count, most)),
            pltpu.SemaphoreType.DMA((count,)),
        ],
        compiler_params=pltpu.CompilerParams(
            collective_id=collective_id, has_side_effects=True, vmem_limit_bytes=VMEM_LIMIT
        ),
        name="exchange_%d" % collective_id,
    )(*[item for item, _, _ in items])


class Group:
    def __init__(self, rows_n, cols_n, far_send, far_recv, near_send, near_recv):
        self.rows_n, self.cols_n = rows_n, cols_n
        self.row, self.col = lax.axis_index("row"), lax.axis_index("col")
        self.me = self.place(0, self.row)
        self.far_send, self.far_recv = far_send, far_recv
        self.near_send, self.near_recv = near_send, near_recv

    def place(self, step, row):
        return lax.rem(self.col + step + self.cols_n, self.cols_n) * self.rows_n + row

    def greet(self):
        barrier = pltpu.get_barrier_semaphore()
        for step in range(1, self.cols_n):
            pl.semaphore_signal(
                barrier,
                inc=1,
                device_id={"col": lax.rem(self.col + step, self.cols_n)},
                device_id_type=MESH,
            )
        pl.semaphore_signal(barrier, inc=1, device_id={"row": 1 - self.row}, device_id_type=MESH)
        pl.semaphore_wait(barrier, self.cols_n)

    def block(self, ref, place, tokens):
        return ref.at[pl.ds(pl.multiple_of(place * tokens, tokens), tokens)]

    def far(self, phase, step, src, dst):
        return pltpu.make_async_remote_copy(
            src_ref=src,
            dst_ref=dst,
            send_sem=self.far_send.at[phase, step - 1],
            recv_sem=self.far_recv.at[phase, step - 1],
            device_id={"col": lax.rem(self.col + step, self.cols_n)},
            device_id_type=MESH,
        )

    def near(self, phase, step, src, dst):
        return pltpu.make_async_remote_copy(
            src_ref=src,
            dst_ref=dst,
            send_sem=self.near_send.at[phase, step],
            recv_sem=self.near_recv.at[phase, step],
            device_id={"row": 1 - self.row},
            device_id_type=MESH,
        )

    def gather_start(self, phase, ref, tokens):
        own = self.block(ref, self.me, tokens)
        for step in range(1, self.cols_n):
            self.far(phase, step, own, own).start()
        self.near(phase, 0, own, own).start()

    def gather_wait(self, phase, ref, tokens):
        own = self.block(ref, self.me, tokens)
        for step in range(1, self.cols_n):
            came = self.block(ref, self.place(-step, self.row), tokens)
            self.far(phase, step, own, came).wait_recv()
            self.near(phase, step, came, came).start()
        for step in range(self.cols_n):
            came = self.block(ref, self.place(-step, self.row), tokens)
            relayed = self.block(ref, self.place(-step, 1 - self.row), tokens)
            self.near(phase, step, came, came).wait_send()
            self.near(phase, step, came, relayed).wait_recv()
        for step in range(1, self.cols_n):
            self.far(phase, step, own, own).wait_send()

    def scatter_near(self, phase, ref, pair, tokens):
        for step in [*range(1, self.cols_n), 0]:
            src = self.block(ref, self.place(step, 1 - self.row), tokens)
            self.near(phase, step, src, pair.at[step]).start()

    def scatter_far(self, phase, ref, pair, landing, tokens):
        for step in range(1, self.cols_n):
            src = self.block(ref, self.place(step, 1 - self.row), tokens)
            self.near(phase, step, src, pair.at[step]).wait_recv()
            mine = self.block(ref, self.place(step, self.row), tokens)
            mine[...] = (mine[...].astype(F32) + pair[step].astype(F32)).astype(BF16)
            self.far(phase, step, mine, landing.at[step - 1]).start()

    def scatter_sum(self, phase, ref, pair, landing, tokens):
        src = self.block(ref, self.place(0, 1 - self.row), tokens)
        self.near(phase, 0, src, pair.at[0]).wait_recv()
        total = self.block(ref, self.me, tokens)[...].astype(F32) + pair[0].astype(F32)
        for step in range(1, self.cols_n):
            mine = self.block(ref, self.place(step, self.row), tokens)
            self.far(phase, step, mine, landing.at[step - 1]).wait_recv()
            total += landing[step - 1].astype(F32)
        for step in range(self.cols_n):
            src = self.block(ref, self.place(step, 1 - self.row), tokens)
            self.near(phase, step, src, pair.at[step]).wait_send()
        for step in range(1, self.cols_n):
            mine = self.block(ref, self.place(step, self.row), tokens)
            self.far(phase, step, mine, landing.at[step - 1]).wait_send()
        return total


def turned(values):
    width = values.shape[1]
    lane = lax.broadcasted_iota(jnp.int32, values.shape, 1)
    first = lax.rem(lane, HEAD_DIM) < HEAD_DIM // 2
    ahead = pltpu.roll(values, width - HEAD_DIM // 2, 1)
    behind = pltpu.roll(values, HEAD_DIM // 2, 1)
    return jnp.where(first, -ahead, behind)


def three_heads(ref, base, group):
    start = base + group * 3 * HEAD_DIM
    return jnp.concatenate(
        [ref[:, start + h * HEAD_DIM : start + (h + 1) * HEAD_DIM] for h in range(3)], axis=0
    )


def probabilities(queries, keys, allowed):
    scores = dot_nt(queries, keys) * HEAD_DIM ** (-0.5)
    scores = jnp.where(allowed, scores, -1e30)
    raised = jnp.exp(scores - jnp.max(scores, axis=1, keepdims=True))
    return raised / jnp.sum(raised, axis=1, keepdims=True)


def allowed_pairs(own_seg, own_tok, all_seg):
    rows, length = own_seg.shape[0], all_seg.shape[1]
    spots = lax.broadcasted_iota(jnp.int32, (rows, length), 1)
    return (own_seg == all_seg) & (spots <= own_tok)


def forward_body(
    rows_n, cols_n,
    x_ref, gain_a, gain_f, wqkv, wout, wgu, wdn, cos, sin, own_seg, own_tok, all_seg,
    y_ref, a_ref, qkv_ref, kv_ref, o_ref, r_ref, b_ref, gu_ref, hid_ref,
    part, pair, landing, *sems,
):
    group = Group(rows_n, cols_n, *sems)
    tokens, width = x_ref.shape
    kv_width = kv_ref.shape[1]
    ff = hid_ref.shape[1]
    group.greet()
    x = x_ref[...]
    scale = lax.rsqrt(jnp.mean(x * x, axis=1, keepdims=True) + EPS)
    a = (x * scale * gain_a[...]).astype(BF16)
    a_ref[...] = a
    raw = dot(a, wqkv[...]).astype(BF16).astype(F32)
    qkv_ref[...] = (raw * cos[...] + turned(raw) * sin[...]).astype(BF16)
    group.block(kv_ref, group.me, tokens)[...] = qkv_ref[:, :kv_width]
    group.gather_start(0, kv_ref, tokens)
    allowed = allowed_pairs(own_seg[...], own_tok[...], all_seg[...])
    group.gather_wait(0, kv_ref, tokens)
    half = kv_width // 2
    for g in range(KV_HEADS):
        keys = kv_ref[:, g * HEAD_DIM : (g + 1) * HEAD_DIM]
        values = kv_ref[:, half + g * HEAD_DIM : half + (g + 1) * HEAD_DIM]
        p = probabilities(three_heads(qkv_ref, kv_width, g), keys, allowed)
        out = dot(p.astype(BF16), values).astype(BF16)
        for h in range(3):
            at = (3 * g + h) * HEAD_DIM
            o_ref[:, at : at + HEAD_DIM] = out[h * tokens : (h + 1) * tokens]
    r = x + dot(o_ref[...], wout[...])
    r_ref[...] = r
    scale = lax.rsqrt(jnp.mean(r * r, axis=1, keepdims=True) + EPS)
    group.block(b_ref, group.me, tokens)[...] = (r * scale * gain_f[...]).astype(BF16)
    group.gather_start(1, b_ref, tokens)
    group.gather_wait(1, b_ref, tokens)
    gu_ref[...] = dot(b_ref[...], wgu[...])
    gate = gu_ref[:, :ff]
    hid_ref[...] = (gate / (1.0 + jnp.exp(-gate)) * gu_ref[:, ff:]).astype(BF16)
    part[...] = dot(hid_ref[...], wdn[...]).astype(BF16)
    group.scatter_near(2, part, pair, tokens)
    group.scatter_far(2, part, pair, landing, tokens)
    y_ref[...] = r_ref[...] + group.scatter_sum(2, part, pair, landing, tokens)


def norm_back(x, gain, gz):
    scale = lax.rsqrt(jnp.mean(x * x, axis=1, keepdims=True) + EPS)
    weighted = gz * gain
    inner = jnp.mean(weighted * x, axis=1, keepdims=True)
    return (
        scale * weighted - x * (scale * scale * scale) * inner,
        jnp.sum(gz * x * scale, axis=0, keepdims=True),
    )


def backward_body(
    rows_n, cols_n,
    gy_ref, x_ref, gain_a, gain_f, wqkv, wout, wgu, wdn, cos, sin, own_seg, own_tok, all_seg,
    a_ref, qkv_ref, kv_ref, o_ref, r_ref, b_ref, gu_ref, hid_ref,
    gx_ref, gwqkv, gwout, gwgu, gwdn, ggain_a, ggain_f,
    gf_ref, ggu_ref, part, pair, landing, kv_part, kv_pair, kv_landing, go_ref, gq_ref, gr_ref,
    *sems,
):
    group = Group(rows_n, cols_n, *sems)
    tokens, width = x_ref.shape
    kv_width = kv_ref.shape[1]
    half = kv_width // 2
    ff = hid_ref.shape[1]
    group.greet()
    group.block(gf_ref, group.me, tokens)[...] = gy_ref[...].astype(BF16)
    group.gather_start(0, gf_ref, tokens)
    group.gather_wait(0, gf_ref, tokens)
    ghid = dot_nt(gf_ref[...], wdn[...])
    gate = gu_ref[:, :ff]
    sig = 1.0 / (1.0 + jnp.exp(-gate))
    ggu_ref[:, :ff] = (ghid * gu_ref[:, ff:] * (sig * (1.0 + gate * (1.0 - sig)))).astype(BF16)
    ggu_ref[:, ff:] = (ghid * (gate * sig)).astype(BF16)
    part[...] = dot_nt(ggu_ref[...], wgu[...]).astype(BF16)
    group.scatter_near(1, part, pair, tokens)
    gwdn[...] = dot_tn(hid_ref[...], gf_ref[...]).astype(BF16)
    group.scatter_far(1, part, pair, landing, tokens)
    gwgu[...] = dot_tn(b_ref[...], ggu_ref[...]).astype(BF16)
    gb = group.scatter_sum(1, part, pair, landing, tokens)
    grad, ggain_f[...] = norm_back(r_ref[...], gain_f[...], gb)
    gr = gy_ref[...] + grad
    gr_ref[...] = gr
    grad_b = gr.astype(BF16)
    go_ref[...] = dot_nt(grad_b, wout[...]).astype(BF16)
    allowed = allowed_pairs(own_seg[...], own_tok[...], all_seg[...])
    factor = HEAD_DIM ** (-0.5)
    gq_ref[...] = jnp.zeros_like(gq_ref)
    for g in range(KV_HEADS):
        keys = kv_ref[:, g * HEAD_DIM : (g + 1) * HEAD_DIM]
        values = kv_ref[:, half + g * HEAD_DIM : half + (g + 1) * HEAD_DIM]
        queries = three_heads(qkv_ref, kv_width, g)
        gout = three_heads(go_ref, 0, g)
        p = probabilities(queries, keys, allowed)
        gp = dot_nt(gout, values)
        gs = (p * (gp - jnp.sum(gp * p, axis=1, keepdims=True))).astype(BF16)
        gq = dot(gs, keys) * factor
        for h in range(3):
            at = kv_width + (3 * g + h) * HEAD_DIM
            gq_ref[:, at : at + HEAD_DIM] = gq[h * tokens : (h + 1) * tokens]
        at = g * HEAD_DIM
        kv_part[:, at : at + HEAD_DIM] = (dot_tn(gs, queries) * factor).astype(BF16)
        kv_part[:, half + at : half + at + HEAD_DIM] = dot_tn(p.astype(BF16), gout).astype(BF16)
    group.scatter_near(2, kv_part, kv_pair, tokens)
    group.scatter_far(2, kv_part, kv_pair, kv_landing, tokens)
    gwout[...] = dot_tn(o_ref[...], gr_ref[...].astype(BF16)).astype(BF16)
    gq_ref[:, :kv_width] = group.scatter_sum(2, kv_part, kv_pair, kv_landing, tokens)
    g0 = gq_ref[...]
    packed = (g0 * cos[...] - turned(g0 * sin[...])).astype(BF16)
    ga = dot_nt(packed, wqkv[...])
    gwqkv[...] = dot_tn(a_ref[...], packed).astype(BF16)
    grad, ggain_a[...] = norm_back(x_ref[...], gain_a[...], ga)
    gx_ref[...] = gr_ref[...] + grad


def call_layer(body, operands, out_shapes, scratch, rows_n, cols_n, phases, collective_id, name):
    spec = pl.BlockSpec(memory_space=pltpu.VMEM)
    return pl.pallas_call(
        functools.partial(body, rows_n, cols_n),
        out_shape=[jax.ShapeDtypeStruct(shape, kind) for shape, kind in out_shapes],
        in_specs=[spec] * len(operands),
        out_specs=[spec] * len(out_shapes),
        scratch_shapes=[pltpu.VMEM(shape, kind) for shape, kind in scratch]
        + [pltpu.SemaphoreType.DMA((phases, cols_n - 1))] * 2
        + [pltpu.SemaphoreType.DMA((phases, cols_n))] * 2,
        compiler_params=pltpu.CompilerParams(
            collective_id=collective_id, has_side_effects=True, vmem_limit_bytes=VMEM_LIMIT
        ),
        name=name,
    )(*operands)


def tables(segment_row, offset, row_count, kv_width, padded, used):
    own_ids = lax.dynamic_slice_in_dim(segment_row, offset, row_count)
    token_ids = offset + jnp.arange(row_count, dtype=jnp.int32)
    starts = jnp.sum((segment_row[None, :] < own_ids[:, None]).astype(jnp.int32), axis=1)
    positions = (token_ids - starts).astype(F32)
    frequency = THETA ** (-jnp.arange(HEAD_DIM // 2, dtype=F32) * 2.0 / HEAD_DIM)
    angles = positions[:, None] * frequency[None, :]
    lanes = jnp.arange(padded)
    turns = (lanes < kv_width // 2) | ((lanes >= kv_width) & (lanes < used))
    repeat = padded // (HEAD_DIM // 2)
    cos = jnp.where(turns[None, :], jnp.tile(jnp.cos(angles), (1, repeat)), 1.0)
    sin = jnp.where(turns[None, :], jnp.tile(jnp.sin(angles), (1, repeat)), 0.0)
    return cos, sin, jnp.tile(own_ids, 3)[:, None], jnp.tile(token_ids, 3)[:, None]


def on_device(
    inputs, segments, cotangent, gain_attn, w_query, w_key, w_value, w_out, gain_ffn,
    w_gate, w_up, w_down,
):
    rows_n, cols_n = lax.axis_size("row"), lax.axis_size("col")
    section = lax.axis_index("section")
    size = rows_n * cols_n
    length = segments.shape[2]
    tokens = length // size
    band = w_query.shape[1]
    width = band * rows_n
    qc, kc = w_query.shape[2], w_key.shape[2]
    kv_width = 2 * kc * cols_n
    used = kv_width + qc * cols_n
    padded = -(-used // 128) * 128
    fc = w_gate.shape[2] // rows_n
    fp = -(-fc // 128) * 128

    qkv = jnp.concatenate([w_key[0], w_value[0], w_query[0]], axis=1)
    gate_up = jnp.stack(
        [w_gate[0].reshape(band, rows_n, fc), w_up[0].reshape(band, rows_n, fc)], axis=2
    ).transpose(1, 0, 2, 3).reshape(rows_n, band, 2 * fc)
    down = w_down[0].reshape(rows_n, fc, band)
    gains = jnp.stack([gain_attn[0], gain_ffn[0]])
    own_qkv, own_out, qkv, out, gate_up, down, gains = exchange(
        [
            (qkv, "col", True), (w_out[0], "col", True),
            (qkv, "section", True), (w_out[0], "section", True), (gate_up, "section", True),
            (down, "section", True), (gains, "section", True),
        ],
        0,
    )

    def other(item):
        return lax.dynamic_index_in_dim(item, 1 - section, 0, False)

    def in_order(own, theirs):
        first = section == 0
        return jnp.stack([jnp.where(first, own, theirs), jnp.where(first, theirs, own)], axis=1)

    qkv, out = exchange([(other(qkv), "col", True), (other(out), "col", True)], 1)
    qkv, out = in_order(own_qkv, qkv), in_order(own_out, out)
    mine = lax.dynamic_index_in_dim(inputs[0], section, 0, False).reshape(rows_n, tokens, band)
    cot = lax.dynamic_index_in_dim(cotangent[0], section, 0, False).reshape(rows_n, tokens, band)
    qkv, out, gate_up, down, gains, mine, cot = exchange(
        [
            (qkv, "row", True), (out, "row", True),
            (gate_up.transpose(1, 0, 2, 3), "row", False),
            (down.transpose(1, 0, 2, 3), "row", False),
            (gains, "row", True), (mine, "row", False), (cot, "row", False),
        ],
        2,
    )
    layers = gains.shape[1]
    pad = jnp.zeros((width, padded - used), BF16)
    full = []
    for n in range(layers):
        part = qkv[:, :, n].transpose(0, 2, 1, 3)
        part = jnp.concatenate(
            [
                part[..., :kc].reshape(width, -1),
                part[..., kc : 2 * kc].reshape(width, -1),
                part[..., 2 * kc :].reshape(width, -1),
                pad,
            ],
            axis=1,
        )
        wout = out[:, :, n].transpose(1, 2, 0, 3).reshape(width, width)
        wgu = jnp.pad(
            gate_up[:, n].reshape(width, 2, fc), ((0, 0), (0, 0), (0, fp - fc))
        ).reshape(width, 2 * fp)
        wdn = jnp.pad(
            down[:, n].transpose(1, 0, 2).reshape(fc, width), ((0, fp - fc), (0, 0))
        )
        gain = gains[:, n].transpose(1, 0, 2).reshape(2, 1, width).astype(F32)
        full.append((gain[0], gain[1], part, wout, wgu, wdn))

    segment_row = lax.dynamic_index_in_dim(segments[0], section, 0, False)
    place = lax.axis_index("col") * rows_n + lax.axis_index("row")
    cos, sin, own_seg, own_tok = tables(
        segment_row, place * tokens, tokens, kv_width, padded, used
    )
    table_set = (cos, sin, own_seg, own_tok, segment_row[None, :])

    entry = mine.transpose(1, 0, 2).reshape(tokens, width).astype(F32)
    saved, acts = [], []
    for n in range(layers):
        y, *kept = call_layer(
            forward_body,
            (entry, *full[n], *table_set),
            [
                ((tokens, width), F32), ((tokens, width), BF16), ((tokens, padded), BF16),
                ((length, kv_width), BF16), ((tokens, width), BF16), ((tokens, width), F32),
                ((length, width), BF16), ((length, 2 * fp), F32), ((length, fp), BF16),
            ],
            [
                ((length, width), BF16), ((cols_n, tokens, width), BF16),
                ((cols_n - 1, tokens, width), BF16),
            ],
            rows_n, cols_n, 3, 3, "layer_forward",
        )
        saved.append((entry, kept))
        acts.append(y.astype(BF16))
        entry = acts[-1].astype(F32)

    grad = cot.transpose(1, 0, 2).reshape(tokens, width).astype(F32)
    grads, weight_grads = [None] * layers, [None] * layers
    for n in reversed(range(layers)):
        entry, kept = saved[n]
        grads[n], *weight_grads[n] = call_layer(
            backward_body,
            (grad, entry, *full[n], *table_set, *kept),
            [
                ((tokens, width), F32), ((width, padded), BF16), ((width, width), BF16),
                ((width, 2 * fp), BF16), ((fp, width), BF16), ((1, width), F32), ((1, width), F32),
            ],
            [
                ((length, width), BF16), ((length, 2 * fp), BF16), ((length, width), BF16),
                ((cols_n, tokens, width), BF16), ((cols_n - 1, tokens, width), BF16),
                ((length, kv_width), BF16), ((cols_n, tokens, kv_width), BF16),
                ((cols_n - 1, tokens, kv_width), BF16), ((tokens, width), BF16),
                ((tokens, padded), F32), ((tokens, width), F32),
            ],
            rows_n, cols_n, 3, 4, "layer_backward",
        )
        grad = grads[n].astype(BF16).astype(F32)

    def qkv_blocks(item):
        key, value, query = (
            item[:, at : at + cols_n * cut].reshape(rows_n, band, cols_n, cut)
            for at, cut in ((0, kc), (kv_width // 2, kc), (kv_width, qc))
        )
        return jnp.concatenate([key, value, query], axis=3).transpose(0, 2, 1, 3)

    g_qkv = jnp.stack([qkv_blocks(item[0]) for item in weight_grads], axis=1)
    out_rows = width // cols_n
    g_out = jnp.stack(
        [
            item[1].reshape(cols_n, out_rows, rows_n, band).transpose(2, 0, 1, 3)
            for item in weight_grads
        ],
        axis=1,
    )
    g_gu = jnp.stack(
        [
            item[2].reshape(rows_n, band, 2, fp)[..., :fc].reshape(rows_n, band, 2 * fc)
            for item in weight_grads
        ],
        axis=1,
    )
    g_dn = jnp.stack(
        [item[3][:fc].reshape(fc, rows_n, band).transpose(1, 0, 2) for item in weight_grads],
        axis=1,
    )
    g_gain = jnp.stack(
        [jnp.stack([item[4], item[5]]).reshape(2, rows_n, band) for item in weight_grads]
    ).transpose(2, 0, 1, 3)
    act = jnp.stack(acts).reshape(layers, tokens, rows_n, band).transpose(2, 0, 1, 3)
    in_grad = jnp.stack(grads).reshape(layers, tokens, rows_n, band).transpose(2, 0, 1, 3)
    g_qkv, g_out, g_gu, g_dn, g_gain, act, in_grad = exchange(
        [(item, "row", False) for item in (g_qkv, g_out, g_gu, g_dn, g_gain, act, in_grad)], 5
    )

    def add(item):
        return jnp.sum(item.astype(F32), axis=0)

    g_qkv, g_out, g_gain = exchange(
        [
            (add(g_qkv).astype(BF16), "section", False),
            (add(g_out).astype(BF16), "section", False),
            (add(g_gain), "section", False),
        ],
        6,
    )
    g_qkv, g_out, g_gain, g_gu, g_dn, act, in_grad = exchange(
        [
            (add(g_qkv).astype(BF16), "col", False), (add(g_out).astype(BF16), "col", False),
            (add(g_gain), "col", True),
            (g_gu.transpose(1, 0, 2, 3), "section", False),
            (g_dn.transpose(1, 0, 2, 3), "section", False),
            (act.transpose(1, 0, 2, 3), "section", False),
            (in_grad.transpose(1, 0, 2, 3), "section", False),
        ],
        7,
    )
    activations = act.reshape((1, 1) + inputs.shape[1:])
    input_grads = in_grad.reshape((1, 1) + inputs.shape[1:])
    g_qkv, g_out, g_gu, g_dn, g_gain = (
        add(item)
        for item in exchange(
            [
                (add(g_qkv).astype(BF16), "dp", True), (add(g_out).astype(BF16), "dp", True),
                (add(g_gu).astype(BF16), "dp", True), (add(g_dn).astype(BF16), "dp", True),
                (add(g_gain), "dp", True),
            ],
            8,
        )
    )
    g_gu = g_gu.reshape(rows_n, band, 2, fc).transpose(2, 1, 0, 3).reshape(2, band, rows_n * fc)
    return (
        activations, input_grads, g_gain[0][None], g_qkv[:, 2 * kc :][None], g_qkv[:, :kc][None],
        g_qkv[:, kc : 2 * kc][None], g_out[None], g_gain[1][None], g_gu[0][None], g_gu[1][None],
        g_dn.reshape(rows_n * fc, band)[None],
    )


def solution(mesh):
    grid = P("section", "row", "col")
    turned_grid = P("section", "col", "row")
    gain = P("section", "row")
    tokens = P("dp", None, "col", "row")
    result = P("section", "dp", None, "col", "row")
    weights = (gain, grid, grid, grid, turned_grid, gain, grid, grid, turned_grid)
    return jax.shard_map(
        on_device,
        mesh=mesh,
        in_specs=(tokens, P("dp", None, None), tokens) + weights,
        out_specs=(result, result) + weights,
        check_vma=False,
    )
```

```python
import functools

import jax
import jax.numpy as jnp
from jax import lax
from jax.experimental import pallas as pl
from jax.experimental.pallas import tpu as pltpu
from jax.sharding import PartitionSpec as P

HEADS = 9
KV_HEADS = 3
HEAD_DIM = 64
EPS = 1e-05
THETA = 100000.0
MESH = pl.DeviceIdType.MESH
F32 = jnp.float32
BF16 = jnp.bfloat16
VMEM_LIMIT = 56 * 1024 * 1024


def dot(left, right):
    return jnp.dot(left, right, preferred_element_type=F32)


def dot_tn(left, right):
    return lax.dot_general(left, right, (((0,), (0,)), ((), ())), preferred_element_type=F32)


def dot_nt(left, right):
    return lax.dot_general(left, right, (((1,), (1,)), ((), ())), preferred_element_type=F32)


def exchange(items, collective_id):
    count = len(items)
    axes = sorted({axis for _, axis, _ in items})
    most = max(lax.axis_size(axis) for axis in axes) - 1

    def body(*refs):
        ins, outs = refs[:count], refs[count : 2 * count]
        send_sem, recv_sem, own_sem = refs[2 * count :]
        barrier = pltpu.get_barrier_semaphore()

        def other(axis, step):
            size = lax.axis_size(axis)
            return lax.rem(lax.axis_index(axis) + step + size, size)

        for axis in axes:
            for step in range(1, lax.axis_size(axis)):
                pl.semaphore_signal(
                    barrier, inc=1, device_id={axis: other(axis, step)}, device_id_type=MESH
                )
        pl.semaphore_wait(barrier, sum(lax.axis_size(axis) - 1 for axis in axes))

        def remote(no, step, slot):
            _, axis, gather = items[no]
            target = other(axis, step)
            return pltpu.make_async_remote_copy(
                src_ref=ins[no] if gather else ins[no].at[target],
                dst_ref=outs[no].at[slot],
                send_sem=send_sem.at[no, step - 1],
                recv_sem=recv_sem.at[no, step - 1],
                device_id={axis: target},
                device_id_type=MESH,
            )

        for no, (_, axis, gather) in enumerate(items):
            for step in range(1, lax.axis_size(axis)):
                remote(no, step, lax.axis_index(axis)).start()
        local = []
        for no, (_, axis, gather) in enumerate(items):
            me = lax.axis_index(axis)
            src = ins[no] if gather else ins[no].at[me]
            local.append(pltpu.make_async_copy(src, outs[no].at[me], own_sem.at[no]))
        for copy in local:
            copy.start()
        for copy in local:
            copy.wait()
        for no, (_, axis, gather) in enumerate(items):
            for step in range(1, lax.axis_size(axis)):
                remote(no, step, lax.axis_index(axis)).wait_send()
                remote(no, step, other(axis, -step)).wait_recv()

    shapes = [
        jax.ShapeDtypeStruct(
            (lax.axis_size(axis),) + item.shape if gather else item.shape, item.dtype
        )
        for item, axis, gather in items
    ]
    spec = pl.BlockSpec(memory_space=pltpu.VMEM)
    return pl.pallas_call(
        body,
        out_shape=shapes,
        in_specs=[spec] * count,
        out_specs=[spec] * count,
        scratch_shapes=[
            pltpu.SemaphoreType.DMA((count, most)),
            pltpu.SemaphoreType.DMA((count, most)),
            pltpu.SemaphoreType.DMA((count,)),
        ],
        compiler_params=pltpu.CompilerParams(
            collective_id=collective_id, has_side_effects=True, vmem_limit_bytes=VMEM_LIMIT
        ),
        name="exchange_%d" % collective_id,
    )(*[item for item, _, _ in items])


class Group:
    def __init__(self, rows_n, cols_n, far_send, far_recv, near_send, near_recv):
        self.rows_n, self.cols_n = rows_n, cols_n
        self.row, self.col = lax.axis_index("row"), lax.axis_index("col")
        self.me = self.place(0, self.row)
        self.far_send, self.far_recv = far_send, far_recv
        self.near_send, self.near_recv = near_send, near_recv

    def place(self, step, row):
        return lax.rem(self.col + step + self.cols_n, self.cols_n) * self.rows_n + row

    def greet(self):
        barrier = pltpu.get_barrier_semaphore()
        for step in range(1, self.cols_n):
            pl.semaphore_signal(
                barrier,
                inc=1,
                device_id={"col": lax.rem(self.col + step, self.cols_n)},
                device_id_type=MESH,
            )
        pl.semaphore_signal(barrier, inc=1, device_id={"row": 1 - self.row}, device_id_type=MESH)
        pl.semaphore_wait(barrier, self.cols_n)

    def block(self, ref, place, tokens):
        return ref.at[pl.ds(pl.multiple_of(place * tokens, tokens), tokens)]

    def far(self, phase, step, src, dst):
        return pltpu.make_async_remote_copy(
            src_ref=src,
            dst_ref=dst,
            send_sem=self.far_send.at[phase, step - 1],
            recv_sem=self.far_recv.at[phase, step - 1],
            device_id={"col": lax.rem(self.col + step, self.cols_n)},
            device_id_type=MESH,
        )

    def near(self, phase, step, src, dst):
        return pltpu.make_async_remote_copy(
            src_ref=src,
            dst_ref=dst,
            send_sem=self.near_send.at[phase, step],
            recv_sem=self.near_recv.at[phase, step],
            device_id={"row": 1 - self.row},
            device_id_type=MESH,
        )

    def gather_start(self, phase, ref, tokens):
        own = self.block(ref, self.me, tokens)
        for step in range(1, self.cols_n):
            self.far(phase, step, own, own).start()
        self.near(phase, 0, own, own).start()

    def gather_wait(self, phase, ref, tokens):
        own = self.block(ref, self.me, tokens)
        for step in range(1, self.cols_n):
            came = self.block(ref, self.place(-step, self.row), tokens)
            self.far(phase, step, own, came).wait_recv()
            self.near(phase, step, came, came).start()
        for step in range(self.cols_n):
            came = self.block(ref, self.place(-step, self.row), tokens)
            relayed = self.block(ref, self.place(-step, 1 - self.row), tokens)
            self.near(phase, step, came, came).wait_send()
            self.near(phase, step, came, relayed).wait_recv()
        for step in range(1, self.cols_n):
            self.far(phase, step, own, own).wait_send()

    def scatter_near(self, phase, ref, pair, tokens):
        for step in [*range(1, self.cols_n), 0]:
            src = self.block(ref, self.place(step, 1 - self.row), tokens)
            self.near(phase, step, src, pair.at[step]).start()

    def scatter_far(self, phase, ref, pair, landing, tokens):
        for step in range(1, self.cols_n):
            src = self.block(ref, self.place(step, 1 - self.row), tokens)
            self.near(phase, step, src, pair.at[step]).wait_recv()
            mine = self.block(ref, self.place(step, self.row), tokens)
            mine[...] = (mine[...].astype(F32) + pair[step].astype(F32)).astype(BF16)
            self.far(phase, step, mine, landing.at[step - 1]).start()

    def scatter_sum(self, phase, ref, pair, landing, tokens):
        src = self.block(ref, self.place(0, 1 - self.row), tokens)
        self.near(phase, 0, src, pair.at[0]).wait_recv()
        total = self.block(ref, self.me, tokens)[...].astype(F32) + pair[0].astype(F32)
        for step in range(1, self.cols_n):
            mine = self.block(ref, self.place(step, self.row), tokens)
            self.far(phase, step, mine, landing.at[step - 1]).wait_recv()
            total += landing[step - 1].astype(F32)
        for step in range(self.cols_n):
            src = self.block(ref, self.place(step, 1 - self.row), tokens)
            self.near(phase, step, src, pair.at[step]).wait_send()
        for step in range(1, self.cols_n):
            mine = self.block(ref, self.place(step, self.row), tokens)
            self.far(phase, step, mine, landing.at[step - 1]).wait_send()
        return total


def turned(values):
    width = values.shape[1]
    lane = lax.broadcasted_iota(jnp.int32, values.shape, 1)
    first = lax.rem(lane, HEAD_DIM) < HEAD_DIM // 2
    ahead = pltpu.roll(values, width - HEAD_DIM // 2, 1)
    behind = pltpu.roll(values, HEAD_DIM // 2, 1)
    return jnp.where(first, -ahead, behind)


def three_heads(ref, base, group):
    start = base + group * 3 * HEAD_DIM
    return jnp.concatenate(
        [ref[:, start + h * HEAD_DIM : start + (h + 1) * HEAD_DIM] for h in range(3)], axis=0
    )


def probabilities(queries, keys, allowed):
    scores = dot_nt(queries, keys) * HEAD_DIM ** (-0.5)
    scores = jnp.where(allowed, scores, -1e30)
    raised = jnp.exp(scores - jnp.max(scores, axis=1, keepdims=True))
    return raised / jnp.sum(raised, axis=1, keepdims=True)


def allowed_pairs(own_seg, own_tok, all_seg):
    rows, length = own_seg.shape[0], all_seg.shape[1]
    spots = lax.broadcasted_iota(jnp.int32, (rows, length), 1)
    return (own_seg == all_seg) & (spots <= own_tok)


def forward_body(
    rows_n, cols_n,
    x_ref, gain_a, gain_f, wqkv, wout, wgu, wdn, cos, sin, own_seg, own_tok, all_seg,
    y_ref, a_ref, qkv_ref, kv_ref, o_ref, r_ref, b_ref, gu_ref, hid_ref,
    part, pair, landing, *sems,
):
    group = Group(rows_n, cols_n, *sems)
    tokens, width = x_ref.shape
    kv_width = kv_ref.shape[1]
    ff = hid_ref.shape[1]
    group.greet()
    x = x_ref[...]
    scale = lax.rsqrt(jnp.mean(x * x, axis=1, keepdims=True) + EPS)
    a = (x * scale * gain_a[...]).astype(BF16)
    a_ref[...] = a
    raw = dot(a, wqkv[...]).astype(BF16).astype(F32)
    qkv_ref[...] = (raw * cos[...] + turned(raw) * sin[...]).astype(BF16)
    group.block(kv_ref, group.me, tokens)[...] = qkv_ref[:, :kv_width]
    group.gather_start(0, kv_ref, tokens)
    allowed = allowed_pairs(own_seg[...], own_tok[...], all_seg[...])
    group.gather_wait(0, kv_ref, tokens)
    half = kv_width // 2
    for g in range(KV_HEADS):
        keys = kv_ref[:, g * HEAD_DIM : (g + 1) * HEAD_DIM]
        values = kv_ref[:, half + g * HEAD_DIM : half + (g + 1) * HEAD_DIM]
        p = probabilities(three_heads(qkv_ref, kv_width, g), keys, allowed)
        out = dot(p.astype(BF16), values).astype(BF16)
        for h in range(3):
            at = (3 * g + h) * HEAD_DIM
            o_ref[:, at : at + HEAD_DIM] = out[h * tokens : (h + 1) * tokens]
    r = x + dot(o_ref[...], wout[...])
    r_ref[...] = r
    scale = lax.rsqrt(jnp.mean(r * r, axis=1, keepdims=True) + EPS)
    group.block(b_ref, group.me, tokens)[...] = (r * scale * gain_f[...]).astype(BF16)
    group.gather_start(1, b_ref, tokens)
    group.gather_wait(1, b_ref, tokens)
    gu_ref[...] = dot(b_ref[...], wgu[...])
    gate = gu_ref[:, :ff]
    hid_ref[...] = (gate / (1.0 + jnp.exp(-gate)) * gu_ref[:, ff:]).astype(BF16)
    part[...] = dot(hid_ref[...], wdn[...]).astype(BF16)
    group.scatter_near(2, part, pair, tokens)
    group.scatter_far(2, part, pair, landing, tokens)
    y_ref[...] = r_ref[...] + group.scatter_sum(2, part, pair, landing, tokens)


def norm_back(x, gain, gz):
    scale = lax.rsqrt(jnp.mean(x * x, axis=1, keepdims=True) + EPS)
    weighted = gz * gain
    inner = jnp.mean(weighted * x, axis=1, keepdims=True)
    return (
        scale * weighted - x * (scale * scale * scale) * inner,
        jnp.sum(gz * x * scale, axis=0, keepdims=True),
    )


def backward_body(
    rows_n, cols_n,
    gy_ref, x_ref, gain_a, gain_f, wqkv, wout, wgu, wdn, cos, sin, own_seg, own_tok, all_seg,
    a_ref, qkv_ref, kv_ref, o_ref, r_ref, b_ref, gu_ref, hid_ref,
    gx_ref, gwqkv, gwout, gwgu, gwdn, ggain_a, ggain_f,
    gf_ref, ggu_ref, part, pair, landing, kv_part, kv_pair, kv_landing, go_ref, gq_ref, gr_ref,
    *sems,
):
    group = Group(rows_n, cols_n, *sems)
    tokens, width = x_ref.shape
    kv_width = kv_ref.shape[1]
    half = kv_width // 2
    ff = hid_ref.shape[1]
    group.greet()
    group.block(gf_ref, group.me, tokens)[...] = gy_ref[...].astype(BF16)
    group.gather_start(0, gf_ref, tokens)
    group.gather_wait(0, gf_ref, tokens)
    ghid = dot_nt(gf_ref[...], wdn[...])
    gate = gu_ref[:, :ff]
    sig = 1.0 / (1.0 + jnp.exp(-gate))
    ggu_ref[:, :ff] = (ghid * gu_ref[:, ff:] * (sig * (1.0 + gate * (1.0 - sig)))).astype(BF16)
    ggu_ref[:, ff:] = (ghid * (gate * sig)).astype(BF16)
    part[...] = dot_nt(ggu_ref[...], wgu[...]).astype(BF16)
    group.scatter_near(1, part, pair, tokens)
    gwdn[...] = dot_tn(hid_ref[...], gf_ref[...]).astype(BF16)
    group.scatter_far(1, part, pair, landing, tokens)
    gwgu[...] = dot_tn(b_ref[...], ggu_ref[...]).astype(BF16)
    gb = group.scatter_sum(1, part, pair, landing, tokens)
    grad, ggain_f[...] = norm_back(r_ref[...], gain_f[...], gb)
    gr = gy_ref[...] + grad
    gr_ref[...] = gr
    grad_b = gr.astype(BF16)
    go_ref[...] = dot_nt(grad_b, wout[...]).astype(BF16)
    allowed = allowed_pairs(own_seg[...], own_tok[...], all_seg[...])
    factor = HEAD_DIM ** (-0.5)
    gq_ref[...] = jnp.zeros_like(gq_ref)
    for g in range(KV_HEADS):
        keys = kv_ref[:, g * HEAD_DIM : (g + 1) * HEAD_DIM]
        values = kv_ref[:, half + g * HEAD_DIM : half + (g + 1) * HEAD_DIM]
        queries = three_heads(qkv_ref, kv_width, g)
        gout = three_heads(go_ref, 0, g)
        p = probabilities(queries, keys, allowed)
        gp = dot_nt(gout, values)
        gs = (p * (gp - jnp.sum(gp * p, axis=1, keepdims=True))).astype(BF16)
        gq = dot(gs, keys) * factor
        for h in range(3):
            at = kv_width + (3 * g + h) * HEAD_DIM
            gq_ref[:, at : at + HEAD_DIM] = gq[h * tokens : (h + 1) * tokens]
        at = g * HEAD_DIM
        kv_part[:, at : at + HEAD_DIM] = (dot_tn(gs, queries) * factor).astype(BF16)
        kv_part[:, half + at : half + at + HEAD_DIM] = dot_tn(p.astype(BF16), gout).astype(BF16)
    group.scatter_near(2, kv_part, kv_pair, tokens)
    group.scatter_far(2, kv_part, kv_pair, kv_landing, tokens)
    gwout[...] = dot_tn(o_ref[...], gr_ref[...].astype(BF16)).astype(BF16)
    gq_ref[:, :kv_width] = group.scatter_sum(2, kv_part, kv_pair, kv_landing, tokens)
    g0 = gq_ref[...]
    packed = (g0 * cos[...] - turned(g0 * sin[...])).astype(BF16)
    ga = dot_nt(packed, wqkv[...])
    gwqkv[...] = dot_tn(a_ref[...], packed).astype(BF16)
    grad, ggain_a[...] = norm_back(x_ref[...], gain_a[...], ga)
    gx_ref[...] = gr_ref[...] + grad


def call_layer(body, operands, out_shapes, scratch, rows_n, cols_n, phases, collective_id, name):
    spec = pl.BlockSpec(memory_space=pltpu.VMEM)
    return pl.pallas_call(
        functools.partial(body, rows_n, cols_n),
        out_shape=[jax.ShapeDtypeStruct(shape, kind) for shape, kind in out_shapes],
        in_specs=[spec] * len(operands),
        out_specs=[spec] * len(out_shapes),
        scratch_shapes=[pltpu.VMEM(shape, kind) for shape, kind in scratch]
        + [pltpu.SemaphoreType.DMA((phases, cols_n - 1))] * 2
        + [pltpu.SemaphoreType.DMA((phases, cols_n))] * 2,
        compiler_params=pltpu.CompilerParams(
            collective_id=collective_id, has_side_effects=True, vmem_limit_bytes=VMEM_LIMIT
        ),
        name=name,
    )(*operands)


def tables(segment_row, offset, row_count, kv_width, padded, used):
    own_ids = lax.dynamic_slice_in_dim(segment_row, offset, row_count)
    token_ids = offset + jnp.arange(row_count, dtype=jnp.int32)
    starts = jnp.sum((segment_row[None, :] < own_ids[:, None]).astype(jnp.int32), axis=1)
    positions = (token_ids - starts).astype(F32)
    frequency = THETA ** (-jnp.arange(HEAD_DIM // 2, dtype=F32) * 2.0 / HEAD_DIM)
    angles = positions[:, None] * frequency[None, :]
    lanes = jnp.arange(padded)
    turns = (lanes < kv_width // 2) | ((lanes >= kv_width) & (lanes < used))
    repeat = padded // (HEAD_DIM // 2)
    cos = jnp.where(turns[None, :], jnp.tile(jnp.cos(angles), (1, repeat)), 1.0)
    sin = jnp.where(turns[None, :], jnp.tile(jnp.sin(angles), (1, repeat)), 0.0)
    return cos, sin, jnp.tile(own_ids, 3)[:, None], jnp.tile(token_ids, 3)[:, None]


def on_device(
    inputs, segments, cotangent, gain_attn, w_query, w_key, w_value, w_out, gain_ffn,
    w_gate, w_up, w_down,
):
    rows_n, cols_n = lax.axis_size("row"), lax.axis_size("col")
    section = lax.axis_index("section")
    size = rows_n * cols_n
    length = segments.shape[2]
    tokens = length // size
    band = w_query.shape[1]
    width = band * rows_n
    qc, kc = w_query.shape[2], w_key.shape[2]
    kv_width = 2 * kc * cols_n
    used = kv_width + qc * cols_n
    padded = -(-used // 128) * 128
    fc = w_gate.shape[2] // rows_n
    fp = -(-fc // 128) * 128

    qkv = jnp.concatenate([w_key[0], w_value[0], w_query[0]], axis=1)
    gate_up = jnp.stack(
        [w_gate[0].reshape(band, rows_n, fc), w_up[0].reshape(band, rows_n, fc)], axis=2
    ).transpose(1, 0, 2, 3).reshape(rows_n, band, 2 * fc)
    down = w_down[0].reshape(rows_n, fc, band)
    gains = jnp.stack([gain_attn[0], gain_ffn[0]])
    own_qkv, own_out, qkv, out, gate_up, down, gains = exchange(
        [
            (qkv, "col", True), (w_out[0], "col", True),
            (qkv, "section", True), (w_out[0], "section", True), (gate_up, "section", True),
            (down, "section", True), (gains, "section", True),
        ],
        0,
    )

    def other(item):
        return lax.dynamic_index_in_dim(item, 1 - section, 0, False)

    def in_order(own, theirs):
        first = section == 0
        return jnp.stack([jnp.where(first, own, theirs), jnp.where(first, theirs, own)], axis=1)

    qkv, out = exchange([(other(qkv), "col", True), (other(out), "col", True)], 1)
    qkv, out = in_order(own_qkv, qkv), in_order(own_out, out)
    mine = lax.dynamic_index_in_dim(inputs[0], section, 0, False).reshape(rows_n, tokens, band)
    cot = lax.dynamic_index_in_dim(cotangent[0], section, 0, False).reshape(rows_n, tokens, band)
    qkv, out, gate_up, down, gains, mine, cot = exchange(
        [
            (qkv, "row", True), (out, "row", True),
            (gate_up.transpose(1, 0, 2, 3), "row", False),
            (down.transpose(1, 0, 2, 3), "row", False),
            (gains, "row", True), (mine, "row", False), (cot, "row", False),
        ],
        2,
    )
    layers = gains.shape[1]
    pad = jnp.zeros((width, padded - used), BF16)
    full = []
    for n in range(layers):
        part = qkv[:, :, n].transpose(0, 2, 1, 3)
        part = jnp.concatenate(
            [
                part[..., :kc].reshape(width, -1),
                part[..., kc : 2 * kc].reshape(width, -1),
                part[..., 2 * kc :].reshape(width, -1),
                pad,
            ],
            axis=1,
        )
        wout = out[:, :, n].transpose(1, 2, 0, 3).reshape(width, width)
        wgu = jnp.pad(
            gate_up[:, n].reshape(width, 2, fc), ((0, 0), (0, 0), (0, fp - fc))
        ).reshape(width, 2 * fp)
        wdn = jnp.pad(
            down[:, n].transpose(1, 0, 2).reshape(fc, width), ((0, fp - fc), (0, 0))
        )
        gain = gains[:, n].transpose(1, 0, 2).reshape(2, 1, width).astype(F32)
        full.append((gain[0], gain[1], part, wout, wgu, wdn))

    segment_row = lax.dynamic_index_in_dim(segments[0], section, 0, False)
    place = lax.axis_index("col") * rows_n + lax.axis_index("row")
    cos, sin, own_seg, own_tok = tables(
        segment_row, place * tokens, tokens, kv_width, padded, used
    )
    table_set = (cos, sin, own_seg, own_tok, segment_row[None, :])

    entry = mine.transpose(1, 0, 2).reshape(tokens, width).astype(F32)
    saved, acts = [], []
    for n in range(layers):
        y, *kept = call_layer(
            forward_body,
            (entry, *full[n], *table_set),
            [
                ((tokens, width), F32), ((tokens, width), BF16), ((tokens, padded), BF16),
                ((length, kv_width), BF16), ((tokens, width), BF16), ((tokens, width), F32),
                ((length, width), BF16), ((length, 2 * fp), F32), ((length, fp), BF16),
            ],
            [
                ((length, width), BF16), ((cols_n, tokens, width), BF16),
                ((cols_n - 1, tokens, width), BF16),
            ],
            rows_n, cols_n, 3, 3, "layer_forward",
        )
        saved.append((entry, kept))
        acts.append(y.astype(BF16))
        entry = acts[-1].astype(F32)

    grad = cot.transpose(1, 0, 2).reshape(tokens, width).astype(F32)
    grads, weight_grads = [None] * layers, [None] * layers
    for n in reversed(range(layers)):
        entry, kept = saved[n]
        grads[n], *weight_grads[n] = call_layer(
            backward_body,
            (grad, entry, *full[n], *table_set, *kept),
            [
                ((tokens, width), F32), ((width, padded), BF16), ((width, width), BF16),
                ((width, 2 * fp), BF16), ((fp, width), BF16), ((1, width), F32), ((1, width), F32),
            ],
            [
                ((length, width), BF16), ((length, 2 * fp), BF16), ((length, width), BF16),
                ((cols_n, tokens, width), BF16), ((cols_n - 1, tokens, width), BF16),
                ((length, kv_width), BF16), ((cols_n, tokens, kv_width), BF16),
                ((cols_n - 1, tokens, kv_width), BF16), ((tokens, width), BF16),
                ((tokens, padded), F32), ((tokens, width), F32),
            ],
            rows_n, cols_n, 3, 4, "layer_backward",
        )
        grad = grads[n].astype(BF16).astype(F32)

    def qkv_blocks(item):
        key, value, query = (
            item[:, at : at + cols_n * cut].reshape(rows_n, band, cols_n, cut)
            for at, cut in ((0, kc), (kv_width // 2, kc), (kv_width, qc))
        )
        return jnp.concatenate([key, value, query], axis=3).transpose(0, 2, 1, 3)

    g_qkv = jnp.stack([qkv_blocks(item[0]) for item in weight_grads], axis=1)
    out_rows = width // cols_n
    g_out = jnp.stack(
        [
            item[1].reshape(cols_n, out_rows, rows_n, band).transpose(2, 0, 1, 3)
            for item in weight_grads
        ],
        axis=1,
    )
    g_gu = jnp.stack(
        [
            item[2].reshape(rows_n, band, 2, fp)[..., :fc].reshape(rows_n, band, 2 * fc)
            for item in weight_grads
        ],
        axis=1,
    )
    g_dn = jnp.stack(
        [item[3][:fc].reshape(fc, rows_n, band).transpose(1, 0, 2) for item in weight_grads],
        axis=1,
    )
    g_gain = jnp.stack(
        [jnp.stack([item[4], item[5]]).reshape(2, rows_n, band) for item in weight_grads]
    ).transpose(2, 0, 1, 3)
    act = jnp.stack(acts).reshape(layers, tokens, rows_n, band).transpose(2, 0, 1, 3)
    in_grad = jnp.stack(grads).reshape(layers, tokens, rows_n, band).transpose(2, 0, 1, 3)
    g_qkv, g_out, g_gu, g_dn, g_gain, act, in_grad = exchange(
        [(item, "row", False) for item in (g_qkv, g_out, g_gu, g_dn, g_gain, act, in_grad)], 5
    )

    def add(item):
        return jnp.sum(item.astype(F32), axis=0)

    def of_layer(item, layer):
        return lax.dynamic_index_in_dim(item, layer, 1, False)

    g_qkv, g_out, g_gain, sent_gu, sent_dn = exchange(
        [
            (add(g_qkv).astype(BF16), "section", False),
            (add(g_out).astype(BF16), "section", False),
            (add(g_gain), "section", False),
            (of_layer(g_gu, 1 - section), "dp", True),
            (of_layer(g_dn, 1 - section), "dp", True),
        ],
        6,
    )
    g_qkv, g_out, g_gain, came_gu, came_dn, g_gu, g_dn, act, in_grad = exchange(
        [
            (add(g_qkv).astype(BF16), "col", False), (add(g_out).astype(BF16), "col", False),
            (add(g_gain), "col", True),
            (add(sent_gu).astype(BF16), "section", True),
            (add(sent_dn).astype(BF16), "section", True),
            (of_layer(g_gu, section), "dp", True),
            (of_layer(g_dn, section), "dp", True),
            (act.transpose(1, 0, 2, 3), "section", False),
            (in_grad.transpose(1, 0, 2, 3), "section", False),
        ],
        7,
    )
    activations = act.reshape((1, 1) + inputs.shape[1:])
    input_grads = in_grad.reshape((1, 1) + inputs.shape[1:])
    g_gu = add(g_gu) + other(came_gu).astype(F32)
    g_dn = add(g_dn) + other(came_dn).astype(F32)
    g_qkv, g_out, g_gain = (
        add(item)
        for item in exchange(
            [
                (add(g_qkv).astype(BF16), "dp", True), (add(g_out).astype(BF16), "dp", True),
                (add(g_gain), "dp", True),
            ],
            8,
        )
    )
    g_gu = g_gu.reshape(rows_n, band, 2, fc).transpose(2, 1, 0, 3).reshape(2, band, rows_n * fc)
    return (
        activations, input_grads, g_gain[0][None], g_qkv[:, 2 * kc :][None], g_qkv[:, :kc][None],
        g_qkv[:, kc : 2 * kc][None], g_out[None], g_gain[1][None], g_gu[0][None], g_gu[1][None],
        g_dn.reshape(rows_n * fc, band)[None],
    )


def solution(mesh):
    grid = P("section", "row", "col")
    turned_grid = P("section", "col", "row")
    gain = P("section", "row")
    tokens = P("dp", None, "col", "row")
    result = P("section", "dp", None, "col", "row")
    weights = (gain, grid, grid, grid, turned_grid, gain, grid, grid, turned_grid)
    return jax.shard_map(
        on_device,
        mesh=mesh,
        in_specs=(tokens, P("dp", None, None), tokens) + weights,
        out_specs=(result, result) + weights,
        check_vma=False,
    )
```
